768 devices in a mesh: grp: 12 (over z), sub: 64 (over y, x, core).
Axes of the slice: x: 4, y: 8, z: 12, core: 2. Of those that a mesh axis runs over, the one named last changes fastest.
Arguments:
- users: bfloat16 [12288, 512], P(('grp', 'sub')), may hold values from -6 to 6
- node_ids: int32 [12288, 14], P(('grp', 'sub')), may hold values from 0 to 65535, as said below
- node_table: bfloat16 [65536, 128], P('sub'), may hold values from -6 to 6
- w_in: bfloat16 [640, 2048], replicated, may hold values from -0.25 to 0.25
- b_in: float32 [2048], replicated, may hold values from -3 to 3
- w_out: float32 [2048], replicated, may hold values from -3.6 to 3.6
- logit_grad: float32 [12288, 14], P(('grp', 'sub')), may hold values from -6 to 6
Outputs:
- user_grad: float32 [12288, 512], P(('grp', 'sub'))
- node_grad: float32 [65536, 128], P('sub')
- w1_grad: float32 [2048, 640], P('sub')
The draws below stay inside these ranges and needn't reach their ends.
Inputs may be any that keep to these rules, and one draw needn't show every extreme that they name: `node_ids`: every id lies in 0 to 65535; the shard of id n is n // 1024. Among the 224 pairs of the rows of one device (aligned blocks of 16 rows), at most 7 lie on one shard, and in every block some shard has exactly 7; one shard has exactly 7 in every block.
All inputs are finite; a program needn't handle non-finite values.
Results may differ from the reference program's by a relative error of at most 0.02.
Values may be sent and summed in bfloat16 or wider, within the bound.
A program may use at most 32 MiB of HBM per device.

```python
import jax
import jax.numpy as jnp
from jax import lax

DU = 512
DN = 128
HID = 2048
K = 14
ROWS_DEV = 16
NODE_DEV = 1024
DIN = 640
ROWS = 12288
NODES = 65536
CAP = 7
N_GRP = 12
N_SUB = 64


def draw_node_ids(key, part):
    key = jax.random.fold_in(key, 11)
    blocks = ROWS // ROWS_DEV
    owner_devices = NODES // NODE_DEV
    pair_count = ROWS_DEV * K
    slot_tally_count = owner_devices * CAP
    heaviest_owner = jax.random.randint(jax.random.fold_in(key, 1), (), 0, owner_devices)

    def one_block(index):
        block_random_key = jax.random.fold_in(key, index + 7)
        random_key_extra, random_key_rating, random_key_sorting, random_key_slots = jax.random.split(block_random_key, 4)
        extra_credit = jax.random.randint(random_key_extra, (owner_devices,), 0, 3)
        extra_credit = jnp.where(jnp.arange(owner_devices) == heaviest_owner, 3, extra_credit)
        slot_holder_device = jnp.arange(slot_tally_count) // CAP
        owner_ratings = extra_credit[slot_holder_device] * (1 << 26) + jax.random.randint(random_key_rating, (slot_tally_count,), 0, 1 << 13) * 8192 + jnp.arange(slot_tally_count)
        unused, picked = lax.top_k(owner_ratings, pair_count)
        chosen = jax.random.permutation(random_key_sorting, slot_holder_device[picked])
        local_index = jax.random.randint(random_key_slots, (pair_count,), 0, NODE_DEV)
        return (chosen * NODE_DEV + local_index).reshape(ROWS_DEV, K)
    drawn = lax.map(one_block, jnp.arange(blocks))
    return drawn.reshape(ROWS, K).astype(jnp.int32)


def block_levels(rng, dims, cuts, smallest, top_value):
    gain, own = 1.0, jax.random.fold_in(rng, 6)
    for dim, blocks in cuts:
        steps = jnp.exp(jax.random.uniform(jax.random.fold_in(own, dim), (blocks,), jnp.float32, smallest / len(cuts), top_value / len(cuts)))
        gain = gain * jnp.repeat(steps, dims[dim] // blocks).reshape([-1 if axis == dim else 1 for axis in range(len(dims))])
    return gain


def scatter_about(own_key, extent, spread, limit, pieces=(), held_as=jnp.bfloat16):
    entries = jax.random.normal(own_key, extent, jnp.float32) * spread
    if len(pieces) > 0:
        entries = block_levels(own_key, extent, pieces, -0.22, 0.18) * entries
    return jnp.clip(entries, min=-limit, max=limit).astype(held_as)


def setup_inputs(seed: int = 0) -> dict:
    splits = jax.random.split(jax.random.key(seed), 8)
    return {
        "users": scatter_about(splits[0], (ROWS, DU), 1.0, 6.0, ((0, 768),)),
        "node_ids": draw_node_ids(jax.random.fold_in(splits[7], 71), 0),
        "node_table": scatter_about(splits[2], (NODES, DN), 1.0, 6.0, ((0, 64),)),
        "w_in": scatter_about(splits[3], (DIN, HID), DIN ** -0.5, 0.25),
        "b_in": scatter_about(splits[4], (HID,), 0.5, 3.0, (), jnp.float32),
        "w_out": scatter_about(splits[5], (HID,), 0.6, 3.6, (), jnp.float32),
        "logit_grad": scatter_about(splits[6], (ROWS, K), 1.0, 6.0, ((0, 768),), jnp.float32),
    }


def reference(users, node_ids, node_table, w_in, b_in, w_out, logit_grad):
    blocks = ROWS // ROWS_DEV
    user_blocks = users.reshape(blocks, ROWS_DEV, DU)
    id_blocks = node_ids.reshape(blocks, ROWS_DEV * K)
    grad_blocks = logit_grad.reshape(blocks, ROWS_DEV * K)

    def pair_block(carry, block):
        node_acc, weight_acc = carry
        block_users, flat_ids, flat_grad = block
        fetched = node_table[flat_ids]
        pair_input = jnp.concatenate([jnp.repeat(block_users, K, axis=0), fetched], axis=1)
        pre_act = jnp.dot(pair_input, w_in, preferred_element_type=jnp.float32) + b_in
        squash = jax.nn.sigmoid(pre_act)
        pre_grad = (flat_grad[:, None] * w_out * squash * (1.0 + pre_act * (1.0 - squash))).astype(jnp.bfloat16)
        pair_grad = jnp.dot(pre_grad, w_in.T, preferred_element_type=jnp.float32).astype(jnp.bfloat16)
        pair_grad = lax.optimization_barrier(pair_grad).astype(jnp.float32)
        user_part = jnp.sum(pair_grad[:, :DU].reshape(ROWS_DEV, K, DU), axis=1)
        node_acc = node_acc.at[flat_ids].add(pair_grad[:, DU:])
        weight_acc = weight_acc + jnp.dot(pre_grad.T, pair_input, preferred_element_type=jnp.float32)
        return (node_acc, weight_acc), user_part

    start_nodes = jnp.zeros((NODES, DN), jnp.float32)
    start_weight = jnp.zeros((HID, DIN), jnp.float32)
    (node_grad, weight_sum), user_parts = lax.scan(pair_block, (start_nodes, start_weight), (user_blocks, id_blocks, grad_blocks))
    user_grad = user_parts.reshape(ROWS, DU)
    w1_grad = weight_sum / float(N_GRP * N_SUB)
    return user_grad, node_grad, w1_grad
```

```python
import functools

import jax
import jax.numpy as jnp
from jax import lax
from jax.experimental import pallas as pl
from jax.experimental.pallas import tpu as pltpu
from jax.sharding import PartitionSpec as P

F32 = jnp.float32
BF16 = jnp.bfloat16
SLOTS = 8


def dot(a, b, ca=1, cb=0):
    return lax.dot_general(a, b, (((ca,), (cb,)), ((), ())), preferred_element_type=F32)


def iota(shape, dim):
    return lax.broadcasted_iota(jnp.int32, shape, dim)


def each(n, fn):
    def step(d, carry):
        fn(d)
        return carry

    lax.fori_loop(1, n, step, 0)


def push(src, dst, send_sem, recv_sem, device):
    return pltpu.make_async_remote_copy(
        src_ref=src,
        dst_ref=dst,
        send_sem=send_sem,
        recv_sem=recv_sem,
        device_id=device,
        device_id_type=pl.DeviceIdType.MESH,
    )


def kernel(
    ny, nx, ng,
    ids_ref, users_ref, lg_ref, b_ref, wout_ref, table_hbm, win_hbm,
    ug_ref, ng_ref, w1_ref,
    table, win, place, base, pgs, pn_ref,
    src1, mid1, out1, src2, mid2, out2, src3, mid3, out3,
    urecv, psend, precv, tsend, trecv, qsend, qrecv,
    znode, rnode, anode, bnode, zw, rw, aw, bw,
    load_sem, x_send, x_recv, y_send, y_recv, z_send, z_recv,
):
    rows, per_row = ids_ref.shape
    nodes = table.shape[0]
    width = table.shape[1]
    hid = win.shape[1]
    du = users_ref.shape[1]
    pairs = rows * per_row
    padded = place.shape[0]
    slots = place.shape[1]
    shards = ny * nx
    hb = hid // shards
    band = nx * hb

    g = lax.axis_index("grp")
    me = lax.axis_index("sub")
    y = me // nx
    x = me % nx

    load_table = pltpu.make_async_copy(table_hbm, table, load_sem.at[0])
    load_win = pltpu.make_async_copy(win_hbm, win, load_sem.at[1])
    load_win.start()
    load_table.start()

    def x_peer(d):
        return {"sub": y * nx + (x + d) % nx}

    def y_peer(d):
        return {"sub": ((y + d) % ny) * nx + x}

    def z_peer(d):
        return {"grp": (g + d) % ng}

    barrier = pltpu.get_barrier_semaphore()

    def greet(peer):
        def go(d):
            pl.semaphore_signal(
                barrier, inc=1, device_id=peer(d), device_id_type=pl.DeviceIdType.MESH
            )

        return go

    each(nx, greet(x_peer))
    each(ny, greet(y_peer))
    each(ng, greet(z_peer))

    lanes = 128
    ids = ids_ref[...]
    cols = jnp.concatenate(
        [jnp.broadcast_to(ids[:, k : k + 1], (rows, lanes)) for k in range(per_row)]
        + [jnp.full((padded - pairs, lanes), -1, jnp.int32)],
        axis=0,
    )
    shift = nodes.bit_length() - 1
    owner = lax.shift_right_arithmetic(cols, jnp.int32(shift))
    local = cols & (nodes - 1)
    lane = iota((padded, lanes), 1)
    hit = (owner == lane).astype(F32)
    before = (iota((padded, padded), 0) > iota((padded, padded), 1)).astype(F32).astype(BF16)
    counts = dot(before, hit.astype(BF16))
    rank = jnp.sum(counts * hit, axis=1, keepdims=True)
    code = owner[:, 0:1].astype(F32) * float(SLOTS) + rank
    chosen = (iota((padded, slots), 1).astype(F32) == code).astype(F32).astype(BF16)
    place[...] = chosen
    half = lanes // 2
    asked = jnp.where(
        lane < half, lax.shift_right_arithmetic(local, jnp.int32(5)) + 1, local & 31
    )
    request = dot(chosen, asked.astype(F32).astype(BF16), 0, 0)
    src1[...] = request.reshape(ny, nx, SLOTS, lanes).astype(BF16)

    pl.semaphore_wait(barrier, (nx - 1) + (ny - 1) + (ng - 1))

    def x_stage(num, src, dst):
        return lambda d: push(
            src((x + d) % nx), dst.at[x], x_send.at[num, d], x_recv.at[num, d], x_peer(d)
        )

    def x_arrival(num, src, dst):
        return lambda d: push(
            src(x), dst.at[(x + nx - d) % nx], x_send.at[num, d], x_recv.at[num, d], x_peer(d)
        )

    def y_stage(num, src, dst):
        return lambda d: push(
            src((y + d) % ny), dst.at[y], y_send.at[num, d], y_recv.at[num, d], y_peer(d)
        )

    def y_arrival(num, src, dst):
        return lambda d: push(
            src(y), dst.at[(y + ny - d) % ny], y_send.at[num, d], y_recv.at[num, d], y_peer(d)
        )

    def z_stage(num, src, dst):
        return lambda d: push(
            src((g + d) % ng), dst.at[g], z_send.at[num, d], z_recv.at[num, d], z_peer(d)
        )

    def z_arrival(num, src, dst):
        return lambda d: push(
            src(g), dst.at[(g + ng - d) % ng], z_send.at[num, d], z_recv.at[num, d], z_peer(d)
        )

    def go(n, make):
        each(n, lambda d: make(d).start())

    def come(n, make):
        each(n, lambda d: make(d).wait_recv())

    def gone(n, make):
        each(n, lambda d: make(d).wait_send())

    def by_x(ref):
        return lambda t: ref.at[:, t]

    def by_lead(ref):
        return lambda t: ref.at[t]

    def whole(ref):
        return lambda t: ref

    go(nx, x_stage(0, by_x(src1), mid1))
    mid1[x] = src1[:, x]
    go(nx, x_stage(1, whole(users_ref), urecv))
    urecv[x] = users_ref[...]
    load_win.wait()
    base[...] = dot(users_ref[...], win[0:du, :]) + b_ref[...]
    come(nx, x_arrival(0, by_x(src1), mid1))
    go(ny, y_stage(0, by_x(mid1), out1))
    out1[y] = mid1[:, y]
    load_table.wait()
    come(ny, y_arrival(0, by_x(mid1), out1))

    wanted = out1[...].astype(F32).reshape(slots, lanes)
    place_of = (wanted[:, 0:1] - 1.0) * 32.0 + wanted[:, half : half + 1]
    select = (iota((slots, nodes), 1).astype(F32) == place_of).astype(F32).astype(BF16)
    fetched = dot(select, table[...])
    src2[...] = fetched.reshape(ny, nx, SLOTS, width).astype(BF16)
    go(nx, x_stage(2, by_x(src2), mid2))
    mid2[x] = src2[:, x]
    come(nx, x_arrival(2, by_x(src2), mid2))
    go(ny, y_stage(1, by_x(mid2), out2))
    out2[y] = mid2[:, y]
    come(ny, y_arrival(1, by_x(mid2), out2))

    returned = out2[...].astype(F32).reshape(slots, width).astype(BF16)
    pn = dot(place[0:pairs, :], returned).astype(BF16)
    pn_ref[...] = pn
    grad_col = jnp.concatenate([lg_ref[:, k : k + 1] for k in range(per_row)], axis=0)
    step = min(hid, 512)
    sums = []
    for c in range(0, hid, step):
        cut = slice(c, c + step)
        part = dot(pn, win[du:, cut]).reshape(per_row, rows, step)
        pre = (part + base[:, cut][None]).reshape(pairs, step)
        squash = jax.nn.sigmoid(pre)
        pre_grad = (
            (grad_col * wout_ref[:, cut]) * (squash * (1.0 + pre * (1.0 - squash)))
        ).astype(BF16)
        pgs[:, cut] = pre_grad
        sums.append(jnp.sum(pre_grad.astype(F32).reshape(per_row, rows, step), axis=0))
    in_grad = dot(pgs[...], win[du:, :], 1, 1).astype(BF16)
    back = dot(place[0:pairs, :], in_grad, 0, 0)

    src3[...] = back.reshape(ny, nx, SLOTS, width).astype(BF16)
    go(nx, x_stage(3, by_x(src3), mid3))
    mid3[x] = src3[:, x]

    row_sum = jnp.concatenate(sums, axis=1)
    turned = jnp.concatenate([row_sum[:, j * band : (j + 1) * band] for j in range(ny)], axis=0).T
    for i in range(nx):
        tsend[i] = turned[i * hb : (i + 1) * hb].astype(BF16)
    for j in range(ny):
        prod = dot(pgs[:, j * band : (j + 1) * band], pn_ref[...], 0, 0).astype(BF16)
        for i in range(nx):
            psend[i, j] = prod[i * hb : (i + 1) * hb]

    come(nx, x_arrival(3, by_x(src3), mid3))
    go(ny, y_stage(2, by_x(mid3), out3))
    out3[y] = mid3[:, y]
    go(nx, x_stage(4, by_lead(tsend), trecv))
    go(nx, x_stage(5, by_lead(psend), precv))
    trecv[x] = tsend[x]
    precv[x] = psend[x]
    ug_ref[...] = dot(row_sum.astype(BF16), win[0:du, :], 1, 1)
    come(ny, y_arrival(2, by_x(mid3), out3))

    arrived = out3[...].astype(F32).reshape(slots, width).astype(BF16)
    node_part = dot(select, arrived, 0, 0).astype(BF16)
    zr = znode.shape[1]
    for j in range(ng):
        lo, hi = min(j * zr, nodes), min((j + 1) * zr, nodes)
        if hi > lo:
            znode[j, 0 : hi - lo] = node_part[lo:hi]
        if hi - lo < zr:
            znode[j, hi - lo :] = jnp.zeros((zr - (hi - lo), width), BF16)
    go(ng, z_stage(0, by_lead(znode), rnode))
    rnode[g] = znode[g]

    come(nx, x_arrival(1, whole(users_ref), urecv))
    come(nx, x_arrival(4, by_lead(tsend), trecv))
    come(nx, x_arrival(5, by_lead(psend), precv))
    node_cols = precv[0].astype(F32)
    for i in range(1, nx):
        node_cols += precv[i].astype(F32)
    tl = trecv.shape[2]
    own_row = iota((ny * hb, tl), 0) // hb == iota((ny * hb, tl), 1) // rows
    keep = own_row.astype(F32).astype(BF16)
    left = jnp.concatenate(
        [jnp.concatenate([trecv[i]] * ny, axis=0) * keep for i in range(nx)], axis=1
    )
    right = jnp.concatenate([urecv[i] for i in range(nx) for _ in range(ny)], axis=0)
    user_cols = dot(left, right)
    for j in range(ny):
        qsend[j, :, 0:du] = user_cols[j * hb : (j + 1) * hb].astype(BF16)
        qsend[j, :, du:] = node_cols[j].astype(BF16)
    go(ny, y_stage(3, by_lead(qsend), qrecv))
    qrecv[y] = qsend[y]
    come(ng, z_arrival(0, by_lead(znode), rnode))
    node_sum = rnode[0].astype(F32)
    for j in range(1, ng):
        node_sum += rnode[j].astype(F32)
    bnode[...] = node_sum.astype(BF16)
    go(ng, z_stage(1, whole(bnode), anode))
    anode[g] = bnode[...]

    come(ny, y_arrival(3, by_lead(qsend), qrecv))
    block = qrecv[0].astype(F32)
    for j in range(1, ny):
        block += qrecv[j].astype(F32)
    block = block.astype(BF16)
    across = (du + width) // lanes
    tiles = [(a, c) for a in range(hb // 16) for c in range(across)]
    per = zw.shape[1] // 16
    for n in range(ng * per):
        at = (n // per, slice((n % per) * 16, (n % per) * 16 + 16))
        if n < len(tiles):
            a, c = tiles[n]
            zw[at] = block[a * 16 : a * 16 + 16, c * lanes : (c + 1) * lanes]
        else:
            zw[at] = jnp.zeros((16, lanes), BF16)
    go(ng, z_stage(2, by_lead(zw), rw))
    rw[g] = zw[g]
    come(ng, z_arrival(2, by_lead(zw), rw))
    tile_sum = rw[0].astype(F32)
    for j in range(1, ng):
        tile_sum += rw[j].astype(F32)
    bw[...] = tile_sum.astype(BF16)
    go(ng, z_stage(3, whole(bw), aw))
    aw[g] = bw[...]

    come(ng, z_arrival(1, whole(bnode), anode))
    for j in range(ng):
        lo, hi = min(j * zr, nodes), min((j + 1) * zr, nodes)
        if hi > lo:
            ng_ref[lo:hi] = anode[j, 0 : hi - lo].astype(F32)
    come(ng, z_arrival(3, whole(bw), aw))
    devices = float(shards * ng)
    for n, (a, c) in enumerate(tiles):
        at = (n // per, slice((n % per) * 16, (n % per) * 16 + 16))
        w1_ref[a * 16 : a * 16 + 16, c * lanes : (c + 1) * lanes] = aw[at].astype(F32) / devices

    gone(nx, x_stage(0, by_x(src1), mid1))
    gone(nx, x_stage(1, whole(users_ref), urecv))
    gone(nx, x_stage(2, by_x(src2), mid2))
    gone(nx, x_stage(3, by_x(src3), mid3))
    gone(nx, x_stage(4, by_lead(tsend), trecv))
    gone(nx, x_stage(5, by_lead(psend), precv))
    gone(ny, y_stage(0, by_x(mid1), out1))
    gone(ny, y_stage(1, by_x(mid2), out2))
    gone(ny, y_stage(2, by_x(mid3), out3))
    gone(ny, y_stage(3, by_lead(qsend), qrecv))
    gone(ng, z_stage(0, by_lead(znode), rnode))
    gone(ng, z_stage(1, whole(bnode), anode))
    gone(ng, z_stage(2, by_lead(zw), rw))
    gone(ng, z_stage(3, whole(bw), aw))


def local(ng, shards, users, node_ids, node_table, w_in, b_in, w_out, logit_grad):
    nx = 8 if shards > 8 and shards % 8 == 0 else 2
    ny = shards // nx
    rows, per_row = node_ids.shape
    du = users.shape[1]
    nodes, width = node_table.shape
    din, hid = w_in.shape
    pairs = rows * per_row
    padded = -(-pairs // 128) * 128
    slots = shards * SLOTS
    hb = hid // shards
    zr = -(-nodes // (ng * 16)) * 16
    tiles = (hb // 16) * (din // 128)
    zt = -(-tiles // ng) * 16
    vmem, hbm = pl.BlockSpec(memory_space=pltpu.VMEM), pl.BlockSpec(memory_space=pl.ANY)

    def ex():
        return [
            pltpu.VMEM((ny, nx, SLOTS, width), BF16),
            pltpu.VMEM((nx, ny, SLOTS, width), BF16),
            pltpu.VMEM((ny, nx, SLOTS, width), BF16),
        ]

    return pl.pallas_call(
        functools.partial(kernel, ny, nx, ng),
        out_shape=(
            jax.ShapeDtypeStruct((rows, du), F32),
            jax.ShapeDtypeStruct((nodes, width), F32),
            jax.ShapeDtypeStruct((hb, din), F32),
        ),
        in_specs=[vmem] * 5 + [hbm] * 2,
        out_specs=(vmem, vmem, vmem),
        scratch_shapes=[
            pltpu.VMEM((nodes, width), BF16),
            pltpu.VMEM((din, hid), BF16),
            pltpu.VMEM((padded, slots), BF16),
            pltpu.VMEM((rows, hid), F32),
            pltpu.VMEM((pairs, hid), BF16),
            pltpu.VMEM((pairs, width), BF16),
            *ex(), *ex(), *ex(),
            pltpu.VMEM((nx, rows, du), BF16),
            pltpu.VMEM((nx, ny, hb, width), BF16),
            pltpu.VMEM((nx, ny, hb, width), BF16),
            pltpu.VMEM((nx, hb, ny * rows), BF16),
            pltpu.VMEM((nx, hb, ny * rows), BF16),
            pltpu.VMEM((ny, hb, din), BF16),
            pltpu.VMEM((ny, hb, din), BF16),
            pltpu.VMEM((ng, zr, width), BF16),
            pltpu.VMEM((ng, zr, width), BF16),
            pltpu.VMEM((ng, zr, width), BF16),
            pltpu.VMEM((zr, width), BF16),
            pltpu.VMEM((ng, zt, 128), BF16),
            pltpu.VMEM((ng, zt, 128), BF16),
            pltpu.VMEM((ng, zt, 128), BF16),
            pltpu.VMEM((zt, 128), BF16),
            pltpu.SemaphoreType.DMA((2,)),
            pltpu.SemaphoreType.DMA((6, nx)),
            pltpu.SemaphoreType.DMA((6, nx)),
            pltpu.SemaphoreType.DMA((4, ny)),
            pltpu.SemaphoreType.DMA((4, ny)),
            pltpu.SemaphoreType.DMA((4, ng)),
            pltpu.SemaphoreType.DMA((4, ng)),
        ],
        compiler_params=pltpu.CompilerParams(
            collective_id=0, has_side_effects=True, vmem_limit_bytes=40 * 2**20
        ),
    )(
        node_ids, users, logit_grad, b_in.reshape(1, hid), w_out.reshape(1, hid),
        node_table, w_in,
    )


def solution(mesh):
    ng, shards = mesh.shape["grp"], mesh.shape["sub"]
    return jax.shard_map(
        functools.partial(local, ng, shards),
        mesh=mesh,
        in_specs=(
            P(("grp", "sub"), None),
            P(("grp", "sub"), None),
            P("sub", None),
            P(),
            P(),
            P(),
            P(("grp", "sub"), None),
        ),
        out_specs=(P(("grp", "sub"), None), P("sub", None), P("sub", None)),
        check_vma=False,
    )
```

```python
import functools

import jax
import jax.numpy as jnp
from jax import lax
from jax.experimental import pallas as pl
from jax.experimental.pallas import tpu as pltpu
from jax.sharding import PartitionSpec as P

F32 = jnp.float32
BF16 = jnp.bfloat16
SLOTS = 8


def dot(a, b, ca=1, cb=0):
    return lax.dot_general(a, b, (((ca,), (cb,)), ((), ())), preferred_element_type=F32)


def iota(shape, dim):
    return lax.broadcasted_iota(jnp.int32, shape, dim)


def each(n, fn):
    def step(d, carry):
        fn(d)
        return carry

    lax.fori_loop(1, n, step, 0)


def push(src, dst, send_sem, recv_sem, device):
    return pltpu.make_async_remote_copy(
        src_ref=src,
        dst_ref=dst,
        send_sem=send_sem,
        recv_sem=recv_sem,
        device_id=device,
        device_id_type=pl.DeviceIdType.MESH,
    )


def kernel(
    ny, nx, ng,
    ids_hbm, users_hbm, lg_hbm, b_hbm, wout_hbm, table_hbm, win_hbm,
    ug_ref, anode, aw,
    ids_ref, users_ref, lg_ref, b_ref, wout_ref, table, win,
    place, place_t, select_t, right, base, pgs,
    src1, out1, src2, out2, src3, out3,
    urecv, psend, precv, tsend, trecv, qusend, qurecv, qnsend, qnrecv,
    znode, nrecv, hsum, frecv, bnode, afar, zw, rw, bw,
    load_sem, own_sem, d_send, d_recv, x_send, x_recv, y_send, y_recv, z_send, z_recv,
    zn_send, zn_recv, zf_send, zf_recv,
):
    rows, per_row = ids_ref.shape
    nodes = table.shape[0]
    width = table.shape[1]
    hid = win.shape[1]
    du = users_ref.shape[1]
    pairs = rows * per_row
    padded = place.shape[0]
    slots = place.shape[1]
    shards = ny * nx
    hb = hid // shards
    band = nx * hb

    g = lax.axis_index("grp")
    me = lax.axis_index("sub")
    y = me // nx
    x = me % nx

    loads = [
        pltpu.make_async_copy(src, dst, load_sem.at[n])
        for n, (src, dst) in enumerate(
            [
                (ids_hbm, ids_ref),
                (users_hbm, users_ref),
                (win_hbm, win),
                (table_hbm, table),
                (b_hbm, b_ref),
                (wout_hbm, wout_ref),
                (lg_hbm, lg_ref),
            ]
        )
    ]
    for load in loads:
        load.start()
    load_ids, load_users, load_win, load_table, *load_small = loads

    def x_peer(d):
        return {"sub": y * nx + (x + d) % nx}

    def y_peer(d):
        return {"sub": ((y + d) % ny) * nx + x}

    def sub_peer(d):
        return {"sub": (me + d) % shards}

    def z_peer(d):
        return {"grp": (g + d) % ng}

    barrier = pltpu.get_barrier_semaphore()

    def greet(peer):
        def go(d):
            pl.semaphore_signal(
                barrier, inc=1, device_id=peer(d), device_id_type=pl.DeviceIdType.MESH
            )

        return go

    each(shards, greet(sub_peer))
    each(ng, greet(z_peer))

    lanes = 128
    half = lanes // 2
    load_ids.wait()
    ids = ids_ref[...]
    cols = jnp.concatenate(
        [jnp.broadcast_to(ids[:, k : k + 1], (rows, lanes)) for k in range(per_row)]
        + [jnp.full((padded - pairs, lanes), -1, jnp.int32)],
        axis=0,
    )
    shift = nodes.bit_length() - 1
    owner = lax.shift_right_arithmetic(cols, jnp.int32(shift))
    local = cols & (nodes - 1)
    lane = iota((padded, lanes), 1)
    hit = (owner == lane).astype(F32)
    hit_low = hit.astype(BF16)
    before = (iota((padded, padded), 0) > iota((padded, padded), 1)).astype(F32).astype(BF16)
    rank = jnp.sum(dot(before, hit_low) * hit, axis=1, keepdims=True)
    slot_lane = rank.astype(jnp.int32)
    high, low = lax.shift_right_arithmetic(local, jnp.int32(5)) + 1, local & 31
    asked = jnp.where(lane == slot_lane, high, jnp.where(lane == slot_lane + half, low, 0))
    request = dot(hit_low, asked.astype(F32).astype(BF16), 0, 0)
    src1[...] = request[0:shards].reshape(shards, 1, lanes)

    pl.semaphore_wait(barrier, (shards - 1) + (ng - 1))

    def x_stage(num, src, dst):
        return lambda d: push(
            src((x + d) % nx), dst.at[x], x_send.at[num, d], x_recv.at[num, d], x_peer(d)
        )

    def x_arrival(num, src, dst):
        return lambda d: push(
            src(x), dst.at[(x + nx - d) % nx], x_send.at[num, d], x_recv.at[num, d], x_peer(d)
        )

    def y_stage(num, src, dst):
        return lambda d: push(
            src((y + d) % ny), dst.at[y], y_send.at[num, d], y_recv.at[num, d], y_peer(d)
        )

    def y_arrival(num, src, dst):
        return lambda d: push(
            src(y), dst.at[(y + ny - d) % ny], y_send.at[num, d], y_recv.at[num, d], y_peer(d)
        )

    def z_stage(num, src, dst):
        return lambda d: push(
            src((g + d) % ng), dst.at[g], z_send.at[num, d], z_recv.at[num, d], z_peer(d)
        )

    def z_arrival(num, src, dst):
        return lambda d: push(
            src(g), dst.at[(g + ng - d) % ng], z_send.at[num, d], z_recv.at[num, d], z_peer(d)
        )

    def d_stage(num, src, dst):
        return lambda d: push(
            src.at[(me + d) % shards], dst.at[me], d_send.at[num], d_recv.at[num], sub_peer(d)
        )

    def d_all(num, src, dst):
        rest = pl.ds(0, shards - 1)
        return push(src.at[rest], dst.at[rest], d_send.at[num], d_recv.at[num], sub_peer(1))

    def go(n, make):
        each(n, lambda d: make(d).start())

    def come(n, make):
        each(n, lambda d: make(d).wait_recv())

    def gone(n, make):
        each(n, lambda d: make(d).wait_send())

    def by_lead(ref):
        return lambda t: ref.at[t]

    def by_part(ref, h, size):
        return lambda t: ref.at[t, h * size : (h + 1) * size]

    def whole(ref):
        return lambda t: ref

    go(shards, d_stage(0, src1, out1))
    out1[me] = src1[me]
    code = owner[:, 0:1].astype(F32) * float(SLOTS) + rank
    chosen = (iota((padded, slots), 1).astype(F32) == code).astype(F32)
    place[...] = chosen.astype(BF16)
    place_t[...] = chosen.T.astype(BF16)
    slot_row = iota((slots, lanes), 0) % SLOTS
    slot_col = iota((slots, lanes), 1)
    weight = jnp.where(slot_col == slot_row, 32.0, 0.0)
    weight = weight + jnp.where(slot_col == slot_row + half, 1.0, 0.0)
    spread = (iota((slots, shards), 0) // SLOTS == iota((slots, shards), 1)).astype(F32)
    load_users.wait()
    go(nx, x_stage(0, whole(users_ref), urecv))
    urecv[x] = users_ref[...]
    load_win.wait()
    for load in load_small:
        load.wait()
    base[...] = dot(users_ref[...], win[0:du, :]) + b_ref[...]
    load_table.wait()
    d_all(0, src1, out1).wait_recv()

    wanted = dot(spread.astype(BF16), out1[...].reshape(shards, lanes).astype(BF16))
    place_of = jnp.sum(wanted * weight, axis=1, keepdims=True) - 32.0
    select = (iota((slots, nodes), 1).astype(F32) == place_of).astype(F32)
    fetched = dot(select.astype(BF16), table[...])
    src2[...] = fetched.reshape(shards, SLOTS, width).astype(BF16)
    go(shards, d_stage(1, src2, out2))
    out2[me] = src2[me]
    select_t[...] = select.T.astype(BF16)
    come(nx, x_arrival(0, whole(users_ref), urecv))
    for i in range(nx):
        for j in range(ny):
            at = (i * ny + j) * rows
            right[at : at + rows] = urecv[i]
    d_all(1, src2, out2).wait_recv()

    returned = out2[...].astype(F32).reshape(slots, width).astype(BF16)
    pn = dot(place[0:pairs, :], returned).astype(BF16)
    grad_col = jnp.concatenate([lg_ref[:, k : k + 1] for k in range(per_row)], axis=0)
    step = min(hid, 512)
    sums = []
    for c in range(0, hid, step):
        cut = slice(c, c + step)
        part = dot(pn, win[du:, cut]).reshape(per_row, rows, step)
        pre = (part + base[:, cut][None]).reshape(pairs, step)
        squash = jax.nn.sigmoid(pre)
        pre_grad = (
            (grad_col * wout_ref[:, cut]) * (squash * (1.0 + pre * (1.0 - squash)))
        ).astype(BF16)
        pgs[:, cut] = pre_grad
        sums.append(jnp.sum(pre_grad.astype(F32).reshape(per_row, rows, step), axis=0))
    in_grad = dot(pgs[...], win[du:, :], 1, 1).astype(BF16)
    back = dot(place_t[:, 0:pairs], in_grad)

    src3[...] = back.reshape(shards, SLOTS, width).astype(BF16)
    go(shards, d_stage(2, src3, out3))
    out3[me] = src3[me]

    row_sum = jnp.concatenate(sums, axis=1)
    turned = jnp.concatenate([row_sum[:, j * band : (j + 1) * band] for j in range(ny)], axis=0).T
    for i in range(nx):
        tsend[i] = turned[i * hb : (i + 1) * hb].astype(BF16)
    go(nx, x_stage(1, by_lead(tsend), trecv))
    trecv[x] = tsend[x]

    pn_t = pn.astype(F32).T.astype(BF16)
    parts = 2 if ny % 2 == 0 else 1
    bands = ny // parts
    for h in range(parts):
        for j in range(h * bands, (h + 1) * bands):
            prod = dot(pn_t, pgs[:, j * band : (j + 1) * band]).T
            for i in range(nx):
                psend[i, j] = prod[i * hb : (i + 1) * hb].astype(BF16)
        go(nx, x_stage(2 + h, by_part(psend, h, bands), precv.at[:, h * bands : (h + 1) * bands]))
    precv[x] = psend[x]

    d_all(2, src3, out3).wait_recv()
    arrived = out3[...].astype(F32).reshape(slots, width).astype(BF16)
    node_part = dot(select_t[...], arrived).reshape(nodes // 8, 8, width).astype(BF16)
    cls, nf, zu = znode.shape[0:3]
    units = nodes // 8
    for o in range(ng):
        lo, hi = min(o * zu, units), min((o + 1) * zu, units)
        if hi > lo:
            znode[o % cls, o // cls, 0 : hi - lo] = node_part[lo:hi]
        if hi - lo < zu:
            znode[o % cls, o // cls, hi - lo :] = jnp.zeros((zu - (hi - lo), 8, width), BF16)
    near = (1, ng - 1) if cls > 1 else ()
    gc, gi = g % cls, g // cls
    order = [f for f in (2, 1, 3) if f < nf] + [f for f in range(4, nf)] + [0]

    def near_to(k):
        return (g + near[k]) % ng

    def near_from(k):
        return (g + ng - near[k]) % ng

    def rs_near(k, f, to):
        there = near_to(k) if to else g
        at = (there // cls + f) % nf
        return push(
            znode.at[there % cls, at], nrecv.at[k, at],
            zn_send.at[0, k, f], zn_recv.at[0, k, f], {"grp": near_to(k)},
        )

    def rs_far(f):
        return push(
            hsum.at[(gi + f) % nf], frecv.at[f],
            zf_send.at[0, f], zf_recv.at[0, f], {"grp": (g + cls * f) % ng},
        )

    def ag_far(f):
        return push(
            bnode, afar.at[f], zf_send.at[1, f], zf_recv.at[1, f], {"grp": (g + cls * f) % ng}
        )

    def ag_near(k, f, to):
        origin = g if to else near_from(k)
        at = (origin // cls + nf - f) % nf
        return push(
            bnode if f == 0 else afar.at[f], anode.at[origin % cls, at],
            zn_send.at[1, k, f], zn_recv.at[1, k, f], {"grp": near_to(k)},
        )

    for f in order:
        for k in range(len(near)):
            rs_near(k, f, True).start()

    come(nx, x_arrival(1, by_lead(tsend), trecv))
    tl = trecv.shape[2]
    own_row = iota((ny * hb, tl), 0) // hb == iota((ny * hb, tl), 1) // rows
    keep = own_row.astype(F32).astype(BF16)
    left = jnp.concatenate(
        [jnp.concatenate([trecv[i]] * ny, axis=0) * keep for i in range(nx)], axis=1
    )
    user_cols = dot(left, right[...]).astype(BF16)
    for j in range(ny):
        qusend[j] = user_cols[j * hb : (j + 1) * hb]
    go(ny, y_stage(0, by_lead(qusend), qurecv))
    qurecv[y] = qusend[y]

    for f in order:
        at = (gi + f) % nf
        mine = znode[gc, at].astype(F32)
        for k in range(len(near)):
            rs_near(k, f, False).wait_recv()
            mine = mine + nrecv[k, at].astype(F32)
        if f > 0:
            hsum[at] = mine.astype(BF16)
            rs_far(f).start()

    for h in range(parts):
        come(nx, x_arrival(2 + h, by_part(psend, h, bands), precv.at[:, h * bands : (h + 1) * bands]))
    for j in range(ny):
        node_cols = precv[0, j].astype(F32)
        for i in range(1, nx):
            node_cols = node_cols + precv[i, j].astype(F32)
        qnsend[j] = node_cols.astype(BF16)
    go(ny, y_stage(1, by_lead(qnsend), qnrecv))
    qnrecv[y] = qnsend[y]

    for f in range(1, nf):
        rs_far(f).wait_recv()
        mine = mine + frecv[f].astype(F32)
    bnode[...] = mine.astype(BF16)
    for f in order[:-1]:
        ag_far(f).start()
    for k in range(len(near)):
        ag_near(k, 0, True).start()
    keep_own = pltpu.make_async_copy(bnode, anode.at[gc, gi], own_sem.at[0])
    keep_own.start()

    ug_ref[...] = dot(row_sum.astype(BF16), win[0:du, :], 1, 1)
    come(ny, y_arrival(0, by_lead(qusend), qurecv))
    come(ny, y_arrival(1, by_lead(qnsend), qnrecv))
    user_block = qurecv[0].astype(F32)
    node_block = qnrecv[0].astype(F32)
    for j in range(1, ny):
        user_block = user_block + qurecv[j].astype(F32)
        node_block = node_block + qnrecv[j].astype(F32)
    block = jnp.concatenate([user_block, node_block], axis=1).astype(BF16)
    tiles = w1_tiles(hb, du + width)
    per = zw.shape[1] // 16
    for n in range(ng * per):
        at = (n // per, slice((n % per) * 16, (n % per) * 16 + 16))
        if n < len(tiles):
            a, c = tiles[n]
            zw[at] = block[a * 16 : a * 16 + 16, c * lanes : (c + 1) * lanes]
        else:
            zw[at] = jnp.zeros((16, lanes), BF16)
    go(ng, z_stage(0, by_lead(zw), rw))
    rw[g] = zw[g]

    keep_far = []
    for f in order[:-1]:
        ag_far(f).wait_recv()
        for k in range(len(near)):
            ag_near(k, f, True).start()
        copy = pltpu.make_async_copy(
            afar.at[f], anode.at[gc, (gi + nf - f) % nf], own_sem.at[1 + f]
        )
        copy.start()
        keep_far.append(copy)

    come(ng, z_arrival(0, by_lead(zw), rw))
    tile_sum = rw[0].astype(F32)
    for j in range(1, ng):
        tile_sum = tile_sum + rw[j].astype(F32)
    bw[...] = tile_sum.astype(BF16)
    go(ng, z_stage(1, whole(bw), aw))
    keep_w = pltpu.make_async_copy(bw, aw.at[g], own_sem.at[1])
    keep_w.start()

    for f in order:
        for k in range(len(near)):
            ag_near(k, f, False).wait_recv()
    come(ng, z_arrival(1, whole(bw), aw))
    keep_own.wait()
    keep_w.wait()
    for copy in keep_far:
        copy.wait()

    for f in order:
        for k in range(len(near)):
            rs_near(k, f, True).wait_send()
            ag_near(k, f, True).wait_send()
    for f in range(1, nf):
        rs_far(f).wait_send()
        ag_far(f).wait_send()
    d_all(0, src1, out1).wait_send()
    d_all(1, src2, out2).wait_send()
    d_all(2, src3, out3).wait_send()
    gone(nx, x_stage(0, whole(users_ref), urecv))
    gone(nx, x_stage(1, by_lead(tsend), trecv))
    for h in range(parts):
        gone(nx, x_stage(2 + h, by_part(psend, h, bands), precv.at[:, h * bands : (h + 1) * bands]))
    gone(ny, y_stage(0, by_lead(qusend), qurecv))
    gone(ny, y_stage(1, by_lead(qnsend), qnrecv))
    gone(ng, z_stage(0, by_lead(zw), rw))
    gone(ng, z_stage(1, whole(bw), aw))


def finish(
    devices, ug_hbm, node_hbm, w1_hbm, ug_out, node_out, w1_out,
    ug, node_in, w1_in, node, w1, in_sem, out_sem,
):
    cls, nf, zu, _, width = node_in.shape
    units, (hb, din) = node.shape[0] // 8, w1.shape
    loads = [
        pltpu.make_async_copy(src, dst, in_sem.at[n])
        for n, (src, dst) in enumerate([(node_hbm, node_in), (w1_hbm, w1_in), (ug_hbm, ug)])
    ]
    stores = [
        pltpu.make_async_copy(src, dst, out_sem.at[n])
        for n, (src, dst) in enumerate([(node, node_out), (w1, w1_out), (ug, ug_out)])
    ]
    for load in loads:
        load.start()
    loads[0].wait()
    for o in range(cls * nf):
        lo, hi = min(o * zu, units), min((o + 1) * zu, units)
        if hi > lo:
            part = node_in[o % cls, o // cls, 0 : hi - lo].astype(F32)
            node[lo * 8 : hi * 8] = part.reshape((hi - lo) * 8, width)
    stores[0].start()
    loads[2].wait()
    stores[2].start()
    loads[1].wait()
    per = w1_in.shape[1] // 16
    for n, (a, c) in enumerate(w1_tiles(hb, din)):
        part = w1_in[n // per, (n % per) * 16 : (n % per) * 16 + 16].astype(F32)
        w1[a * 16 : a * 16 + 16, c * 128 : (c + 1) * 128] = part / devices
    stores[1].start()
    for store in stores:
        store.wait()


def w1_tiles(hb, din):
    return [(a, c) for a in range(hb // 16) for c in range(din // 128)]


def local(ng, shards, users, node_ids, node_table, w_in, b_in, w_out, logit_grad):
    nx = 8 if shards > 8 and shards % 8 == 0 else 2
    ny = shards // nx
    rows, per_row = node_ids.shape
    du = users.shape[1]
    nodes, width = node_table.shape
    din, hid = w_in.shape
    pairs = rows * per_row
    padded = -(-pairs // 128) * 128
    slots = shards * SLOTS
    hb = hid // shards
    cls = 3 if ng % 3 == 0 and ng > 3 else 1
    nf = ng // cls
    zu = -(-nodes // (ng * 8))
    kn = 2 if cls > 1 else 1
    zt = -(-len(w1_tiles(hb, din)) // ng) * 16
    vmem, hbm = pl.BlockSpec(memory_space=pltpu.VMEM), pl.BlockSpec(memory_space=pltpu.HBM)

    parts = pl.pallas_call(
        functools.partial(kernel, ny, nx, ng),
        out_shape=(
            jax.ShapeDtypeStruct((rows, du), F32),
            jax.ShapeDtypeStruct((cls, nf, zu, 8, width), BF16),
            jax.ShapeDtypeStruct((ng, zt, 128), BF16),
        ),
        in_specs=[hbm] * 7,
        out_specs=(vmem, hbm, hbm),
        scratch_shapes=[
            pltpu.VMEM((rows, per_row), jnp.int32),
            pltpu.VMEM((rows, du), BF16),
            pltpu.VMEM((rows, per_row), F32),
            pltpu.VMEM((1, hid), F32),
            pltpu.VMEM((1, hid), F32),
            pltpu.VMEM((nodes, width), BF16),
            pltpu.VMEM((din, hid), BF16),
            pltpu.VMEM((padded, slots), BF16),
            pltpu.VMEM((slots, padded), BF16),
            pltpu.VMEM((nodes, slots), BF16),
            pltpu.VMEM((shards * rows, du), BF16),
            pltpu.VMEM((rows, hid), F32),
            pltpu.VMEM((pairs, hid), BF16),
            *[pltpu.VMEM((shards, 1, 128), F32)] * 2,
            *[pltpu.VMEM((shards, SLOTS, width), BF16)] * 4,
            pltpu.VMEM((nx, rows, du), BF16),
            *[pltpu.VMEM((nx, ny, hb, width), BF16)] * 2,
            *[pltpu.VMEM((nx, hb, ny * rows), BF16)] * 2,
            *[pltpu.VMEM((ny, hb, du), BF16)] * 2,
            *[pltpu.VMEM((ny, hb, width), BF16)] * 2,
            pltpu.VMEM((cls, nf, zu, 8, width), BF16),
            pltpu.VMEM((kn, nf, zu, 8, width), BF16),
            pltpu.VMEM((nf, zu, 8, width), BF16),
            pltpu.VMEM((nf, zu, 8, width), BF16),
            pltpu.VMEM((zu, 8, width), BF16),
            pltpu.VMEM((nf, zu, 8, width), BF16),
            pltpu.VMEM((ng, zt, 128), BF16),
            pltpu.VMEM((ng, zt, 128), BF16),
            pltpu.VMEM((zt, 128), BF16),
            pltpu.SemaphoreType.DMA((7,)),
            pltpu.SemaphoreType.DMA((1 + nf,)),
            pltpu.SemaphoreType.DMA((3,)),
            pltpu.SemaphoreType.DMA((3,)),
            pltpu.SemaphoreType.DMA((4, nx)),
            pltpu.SemaphoreType.DMA((4, nx)),
            pltpu.SemaphoreType.DMA((2, ny)),
            pltpu.SemaphoreType.DMA((2, ny)),
            pltpu.SemaphoreType.DMA((2, ng)),
            pltpu.SemaphoreType.DMA((2, ng)),
            pltpu.SemaphoreType.DMA((2, kn, nf)),
            pltpu.SemaphoreType.DMA((2, kn, nf)),
            pltpu.SemaphoreType.DMA((2, nf)),
            pltpu.SemaphoreType.DMA((2, nf)),
        ],
        compiler_params=pltpu.CompilerParams(
            collective_id=0, has_side_effects=True, vmem_limit_bytes=60 * 2**20
        ),
    )(
        node_ids, users, logit_grad, b_in.reshape(1, hid), w_out.reshape(1, hid),
        node_table, w_in,
    )
    return pl.pallas_call(
        functools.partial(finish, float(shards * ng)),
        out_shape=(
            jax.ShapeDtypeStruct((rows, du), F32),
            jax.ShapeDtypeStruct((nodes, width), F32),
            jax.ShapeDtypeStruct((hb, din), F32),
        ),
        in_specs=[hbm] * 3,
        out_specs=(hbm, hbm, hbm),
        scratch_shapes=[
            pltpu.VMEM((rows, du), F32),
            pltpu.VMEM((cls, nf, zu, 8, width), BF16),
            pltpu.VMEM((ng, zt, 128), BF16),
            pltpu.VMEM((nodes, width), F32),
            pltpu.VMEM((hb, din), F32),
            pltpu.SemaphoreType.DMA((3,)),
            pltpu.SemaphoreType.DMA((3,)),
        ],
        compiler_params=pltpu.CompilerParams(vmem_limit_bytes=60 * 2**20),
    )(*parts)


def solution(mesh):
    ng, shards = mesh.shape["grp"], mesh.shape["sub"]
    return jax.shard_map(
        functools.partial(local, ng, shards),
        mesh=mesh,
        in_specs=(
            P(("grp", "sub"), None),
            P(("grp", "sub"), None),
            P("sub", None),
            P(),
            P(),
            P(),
            P(("grp", "sub"), None),
        ),
        out_specs=(P(("grp", "sub"), None), P("sub", None), P("sub", None)),
        check_vma=False,
    )
```

```python
import functools

import jax
import jax.numpy as jnp
from jax import lax
from jax.experimental import pallas as pl
from jax.experimental.pallas import tpu as pltpu
from jax.sharding import PartitionSpec as P

F32 = jnp.float32
BF16 = jnp.bfloat16
SLOTS = 8


def dot(a, b, ca=1, cb=0):
    return lax.dot_general(a, b, (((ca,), (cb,)), ((), ())), preferred_element_type=F32)


def iota(shape, dim):
    return lax.broadcasted_iota(jnp.int32, shape, dim)


def each(n, fn):
    group = 7 if n > 8 and (n - 1) % 7 == 0 else 1

    def step(i, carry):
        for j in range(group):
            fn(i * group + j + 1)
        return carry

    lax.fori_loop(0, (n - 1) // group, step, 0)


def push(src, dst, send_sem, recv_sem, device):
    return pltpu.make_async_remote_copy(
        src_ref=src,
        dst_ref=dst,
        send_sem=send_sem,
        recv_sem=recv_sem,
        device_id=device,
        device_id_type=pl.DeviceIdType.MESH,
    )


def kernel(
    ny, nx, ng,
    ids_hbm, users_hbm, lg_hbm, b_hbm, wout_hbm, table_hbm, win_hbm,
    ug_out, anode, aw,
    ids_ref, users_ref, lg_ref, b_ref, wout_ref, table, win,
    place, place_t, select_t, base, pgs, weights, spread, ug,
    src1, out1, src2, out2, src3, out3,
    ucol, ssend, srecv, qusend, qurecv, psend, pswap, pdir, pin,
    znode, rrel, rdir, hsum, bnode, afar, zw, rw, bw,
    load_sem, own_sem, d_send, d_recv, y_send, y_recv, c_send, c_recv, s_send, s_recv,
    u_send, u_recv, p_send, p_recv, z_send, z_recv, zn_send, zn_recv,
):
    rows, per_row = ids_ref.shape
    nodes = table.shape[0]
    width = table.shape[1]
    hid = win.shape[1]
    du = users_ref.shape[1]
    pairs = rows * per_row
    padded = place.shape[0]
    slots = place.shape[1]
    shards = ny * nx
    hb = hid // shards
    band = nx * hb

    g = lax.axis_index("grp")
    me = lax.axis_index("sub")
    y = me // nx
    x = me % nx
    c = x % 2
    xch = x // 2
    nxc = nx // 2
    chips = ny * nxc
    chip = me // 2
    q = y * 2 + c

    loads = [
        pltpu.make_async_copy(src, dst, load_sem.at[n])
        for n, (src, dst) in enumerate(
            [
                (ids_hbm, ids_ref),
                (users_hbm, users_ref),
                (win_hbm, win),
                (table_hbm, table),
                (b_hbm, b_ref),
                (wout_hbm, wout_ref),
                (lg_hbm, lg_ref),
            ]
        )
    ]
    for load in loads:
        load.start()
    load_ids, load_users, load_win, load_table, *load_small = loads

    def y_peer(d):
        return {"sub": ((y + d) % ny) * nx + x}

    partner = {"sub": chip * 2 + 1 - c}

    def sub_peer(d):
        return {"sub": (me + d) % shards}

    def z_peer(d):
        return {"grp": (g + d) % ng}

    barrier = pltpu.get_barrier_semaphore()

    def greet(peer):
        def go(d):
            pl.semaphore_signal(
                barrier, inc=1, device_id=peer(d), device_id_type=pl.DeviceIdType.MESH
            )

        return go

    each(shards, greet(sub_peer))
    each(ng, greet(z_peer))

    lanes = 128
    half = lanes // 2
    before = (iota((padded, padded), 0) > iota((padded, padded), 1)).astype(F32).astype(BF16)
    slot_row = iota((slots, lanes), 0) % SLOTS
    slot_col = iota((slots, lanes), 1)
    weight = jnp.where(slot_col == slot_row, 32.0, 0.0)
    weights[...] = weight + jnp.where(slot_col == slot_row + half, 1.0, 0.0)
    spread[...] = (
        (iota((slots, shards), 0) // SLOTS == iota((slots, shards), 1)).astype(F32).astype(BF16)
    )
    load_ids.wait()
    ids = ids_ref[...]
    cols = jnp.concatenate(
        [jnp.broadcast_to(ids[:, k : k + 1], (rows, lanes)) for k in range(per_row)]
        + [jnp.full((padded - pairs, lanes), -1, jnp.int32)],
        axis=0,
    )
    shift = nodes.bit_length() - 1
    owner = lax.shift_right_arithmetic(cols, jnp.int32(shift))
    local = cols & (nodes - 1)
    lane = iota((padded, lanes), 1)
    hit = (owner == lane).astype(F32)
    hit_low = hit.astype(BF16)
    rank = jnp.sum(dot(before, hit_low) * hit, axis=1, keepdims=True)
    slot_lane = rank.astype(jnp.int32)
    high, low = lax.shift_right_arithmetic(local, jnp.int32(5)) + 1, local & 31
    asked = jnp.where(lane == slot_lane, high, jnp.where(lane == slot_lane + half, low, 0))
    request = dot(hit_low, asked.astype(F32).astype(BF16), 0, 0)
    src1[...] = request[0:shards].reshape(shards, 1, lanes)

    pl.semaphore_wait(barrier, (shards - 1) + (ng - 1))

    def y_stage(num, src, dst):
        return lambda d: push(
            src((y + d) % ny), dst.at[y], y_send.at[num, d], y_recv.at[num, d], y_peer(d)
        )

    def y_arrival(num, src, dst):
        return lambda d: push(
            src(y), dst.at[(y + ny - d) % ny], y_send.at[num, d], y_recv.at[num, d], y_peer(d)
        )

    def z_stage(num, src, dst):
        return lambda d: push(
            src((g + d) % ng), dst.at[g], z_send.at[num, d], z_recv.at[num, d], z_peer(d)
        )

    def z_arrival(num, src, dst):
        return lambda d: push(
            src(g), dst.at[(g + ng - d) % ng], z_send.at[num, d], z_recv.at[num, d], z_peer(d)
        )

    def d_stage(num, src, dst):
        return lambda d: push(
            src.at[(me + d) % shards], dst.at[me], d_send.at[num], d_recv.at[num], sub_peer(d)
        )

    def d_all(num, src, dst):
        rest = pl.ds(0, shards - 1)
        return push(src.at[rest], dst.at[rest], d_send.at[num], d_recv.at[num], sub_peer(1))

    def go(n, make):
        each(n, lambda d: make(d).start())

    def come(n, make):
        each(n, lambda d: make(d).wait_recv())

    def gone(n, make):
        each(n, lambda d: make(d).wait_send())

    def by_lead(ref):
        return lambda t: ref.at[t]

    def whole(ref):
        return lambda t: ref

    go(shards, d_stage(0, src1, out1))
    out1[me] = src1[me]

    load_users.wait()
    go(ny, y_stage(0, whole(users_ref), ucol.at[:, c]))
    ucol[y, c] = users_ref[...]
    load_win.wait()
    for load in load_small:
        load.wait()
    base[...] = dot(users_ref[...], win[0:du, :]) + b_ref[...]
    load_table.wait()
    d_all(0, src1, out1).wait_recv()

    wanted = dot(spread[...], out1[...].reshape(shards, lanes).astype(BF16))
    place_of = jnp.sum(wanted * weights[...], axis=1, keepdims=True) - 32.0
    select = (iota((slots, nodes), 1).astype(F32) == place_of).astype(F32)
    fetched = dot(select.astype(BF16), table[...])
    src2[...] = fetched.reshape(shards, SLOTS, width).astype(BF16)
    go(shards, d_stage(1, src2, out2))
    out2[me] = src2[me]
    place_row = jnp.broadcast_to(place_of, (slots, lanes)).T[0:1]
    select_t[...] = (iota((nodes, slots), 0).astype(F32) == place_row).astype(F32).astype(BF16)
    code = owner.astype(F32) * float(SLOTS) + rank
    chosen = (iota((padded, slots), 1).astype(F32) == code[:, 0:1]).astype(F32)
    place[...] = chosen.astype(BF16)
    code_row = code.T[0:1]
    place_t[...] = (iota((slots, padded), 0).astype(F32) == code_row).astype(F32).astype(BF16)
    come(ny, y_arrival(0, whole(users_ref), ucol.at[:, c]))
    swap_users = push(ucol.at[:, c], ucol.at[:, c], c_send.at[0], c_recv.at[0], partner)
    swap_users.start()
    d_all(1, src2, out2).wait_recv()

    returned = out2[...].astype(F32).reshape(slots, width).astype(BF16)
    pn = dot(place[0:pairs, :], returned).astype(BF16)
    grad_col = jnp.concatenate([lg_ref[:, k : k + 1] for k in range(per_row)], axis=0)
    step = min(hid, 512)
    sums = []
    for left in range(0, hid, step):
        cut = slice(left, left + step)
        part = dot(pn, win[du:, cut]).reshape(per_row, rows, step)
        pre = (part + base[:, cut][None]).reshape(pairs, step)
        squash = jax.nn.sigmoid(pre)
        pre_grad = (
            (grad_col * wout_ref[:, cut]) * (squash * (1.0 + pre * (1.0 - squash)))
        ).astype(BF16)
        pgs[:, cut] = pre_grad
        sums.append(jnp.sum(pre_grad.astype(F32).reshape(per_row, rows, step), axis=0))
    in_grad = dot(pgs[...], win[du:, :], 1, 1).astype(BF16)
    back = dot(place_t[:, 0:pairs], in_grad)

    src3[...] = back.reshape(shards, SLOTS, width).astype(BF16)
    go(shards, d_stage(2, src3, out3))
    out3[me] = src3[me]

    row_sum = jnp.concatenate(sums, axis=1)
    bh = band // 2
    for i in range(2 * ny):
        ssend[i] = row_sum[:, i * bh : (i + 1) * bh].astype(BF16)

    def s_stage(d):
        t = (q + d) % (2 * ny)
        return push(
            ssend.at[t], srecv.at[q], s_send.at[d], s_recv.at[d],
            {"sub": (t // 2) * nx + xch * 2 + t % 2},
        )

    def s_arrival(d):
        return push(
            ssend.at[q], srecv.at[(q + 2 * ny - d) % (2 * ny)], s_send.at[d], s_recv.at[d], partner
        )

    go(2 * ny, s_stage)
    srecv[q] = ssend[q]

    pn_t = pn.astype(F32).T.astype(BF16)
    parts = 2 if ny % 2 == 0 else 1
    bands = ny // parts

    def p_swap(h):
        part = slice(h * bands, (h + 1) * bands)
        return push(
            psend.at[1 - c, part], pswap.at[part], c_send.at[1 + h], c_recv.at[1 + h], partner
        )

    for h in range(parts):
        for j in range(h * bands, (h + 1) * bands):
            prod = dot(pn_t, pgs[:, j * band : (j + 1) * band]).T.astype(BF16)
            for i in range(nx):
                psend[i % 2, j, i // 2] = prod[i * hb : (i + 1) * hb]
        p_swap(h).start()
    for h in range(parts):
        p_swap(h).wait_recv()
        part = slice(h * bands, (h + 1) * bands)
        mine = psend[c, part].astype(F32) + pswap[part].astype(F32)
        pdir[h * bands * nxc : (h + 1) * bands * nxc] = mine.reshape(
            bands * nxc, hb, width
        ).astype(BF16)

    def p_stage(d):
        t = (chip + d) % chips
        return push(
            pdir.at[t], pin.at[chip], p_send.at[d], p_recv.at[d], {"sub": t * 2 + c}
        )

    def p_arrival(d):
        return push(
            pdir.at[chip], pin.at[(chip + chips - d) % chips], p_send.at[d], p_recv.at[d], partner
        )

    go(chips, p_stage)
    pin[chip] = pdir[chip]

    swap_users.wait_recv()
    come(2 * ny, s_arrival)
    user_cols = dot(
        srecv[...].reshape(2 * ny * rows, bh), ucol[...].reshape(2 * ny * rows, du), 0, 0
    ).astype(BF16)
    for m in range(nxc):
        qusend[m] = user_cols[m * hb : (m + 1) * hb]

    def u_stage(m):
        at = (xch + m) % nxc
        return push(
            qusend.at[at], qurecv.at[xch], u_send.at[at], u_recv.at[xch],
            {"sub": y * nx + c * nxc + at},
        )

    def u_arrival(i):
        return push(qusend.at[0], qurecv.at[i], u_send.at[0], u_recv.at[i], partner)

    for m in range(nxc):
        at = (xch + m) % nxc

        @pl.when(c * nxc + at != x)
        def _():
            u_stage(m).start()

        @pl.when(c * nxc + at == x)
        def _():
            qurecv[xch] = qusend[at]

    d_all(2, src3, out3).wait_recv()
    arrived = out3[...].astype(F32).reshape(slots, width).astype(BF16)
    node_part = dot(select_t[...], arrived).reshape(nodes // 8, 8, width).astype(BF16)
    zu = znode.shape[1]
    units = nodes // 8
    for o in range(ng):
        lo, hi = min(o * zu, units), min((o + 1) * zu, units)
        if hi > lo:
            znode[o, 0 : hi - lo] = node_part[lo:hi]
        if hi - lo < zu:
            znode[o, hi - lo :] = jnp.zeros((zu - (hi - lo), 8, width), BF16)
    far = ng // 2
    relay = far // 2
    near_by = [(i, k) for k in range(relay - 1, 0, -1) for i in (0, 1)]
    beyond = [(i, k) for k in range(far - 1, relay, -1) for i in (0, 1)]

    def off(i, k):
        return (g + k * (1 - 2 * i) + ng) % ng

    def z_push(phase, i, k, src, dst, hop):
        return push(
            src, dst, zn_send.at[phase, i, k], zn_recv.at[phase, i, k], {"grp": off(i, hop)}
        )

    def rs_to_relay(i, k):
        return z_push(0, i, k, znode.at[off(i, -k)], rrel.at[i, k], relay - k)

    def rs_direct(i, k):
        return z_push(0, i, k, znode.at[off(i, -k)], rdir.at[i, k], -k)

    def rs_relay(i):
        return z_push(0, i, relay, hsum.at[i], rdir.at[i, relay], -relay)

    def ag_direct(i, k):
        return z_push(1, i, k, bnode, anode.at[g], k)

    def ag_to_relay(i):
        return z_push(1, i, relay, bnode, afar.at[i], relay)

    def ag_from_relay(i, k):
        return z_push(1, i, k, afar.at[i], anode.at[off(i, -relay)], k - relay)

    def ag_arrival(i, k):
        return z_push(1, i, k, bnode, anode.at[off(i, -k)], k)

    rs_to_relay(c, far).start()
    for i, k in beyond:
        rs_to_relay(i, k).start()
    for i, k in near_by:
        rs_direct(i, k).start()

    for turn in (1, 0):
        i = (c + turn) % 2
        part = znode[off(i, -relay)].astype(F32)
        for k in range(relay + 1, far + (1 - turn)):
            rs_to_relay(i, k).wait_recv()
            part = part + rrel[i, k].astype(F32)
        hsum[i] = part.astype(BF16)
        rs_relay(i).start()

    come(chips, p_arrival)
    for m in range(nxc):

        @pl.when(m * 2 + x // nxc != x)
        def _():
            u_arrival(m).wait_recv()

    user_block = qurecv[0].astype(F32)
    for j in range(1, nxc):
        user_block = user_block + qurecv[j].astype(F32)
    node_block = pin[0].astype(F32)
    for j in range(1, chips):
        node_block = node_block + pin[j].astype(F32)
    block = jnp.concatenate([user_block, node_block], axis=1).astype(BF16)
    tiles = w1_tiles(hb, du + width)
    per = zw.shape[1] // 16
    for n in range(ng * per):
        at = (n // per, slice((n % per) * 16, (n % per) * 16 + 16))
        if n < len(tiles):
            down, over = tiles[n]
            zw[at] = block[down * 16 : down * 16 + 16, over * lanes : (over + 1) * lanes]
        else:
            zw[at] = jnp.zeros((16, lanes), BF16)
    go(ng, z_stage(0, by_lead(zw), rw))
    rw[g] = zw[g]

    mine = znode[g].astype(F32)
    for i, k in [(i, k) for k in range(1, relay + 1) for i in (0, 1)]:
        rs_direct(i, k).wait_recv()
        mine = mine + rdir[i, k].astype(F32)
    bnode[...] = mine.astype(BF16)
    for i in (0, 1):
        ag_to_relay(i).start()
    for i, k in near_by:
        ag_direct(i, k).start()
    keep_own = pltpu.make_async_copy(bnode, anode.at[g], own_sem.at[0])
    keep_own.start()

    come(ng, z_arrival(0, by_lead(zw), rw))
    tile_sum = rw[0].astype(F32)
    for j in range(1, ng):
        tile_sum = tile_sum + rw[j].astype(F32)
    bw[...] = tile_sum.astype(BF16)
    go(ng, z_stage(1, whole(bw), aw))
    keep_w = pltpu.make_async_copy(bw, aw.at[g], own_sem.at[1])
    keep_w.start()

    keep_far = []
    for turn in (0, 1):
        i = (c + turn) % 2
        ag_to_relay(i).wait_recv()
        for k in range(far - turn, relay, -1):
            ag_from_relay(i, k).start()
        copy = pltpu.make_async_copy(afar.at[i], anode.at[off(i, -relay)], own_sem.at[2 + turn])
        copy.start()
        keep_far.append(copy)

    ug[...] = dot(row_sum.astype(BF16), win[0:du, :], 1, 1)
    keep_ug = pltpu.make_async_copy(ug, ug_out, load_sem.at[0])
    keep_ug.start()
    for i, k in near_by[::-1] + beyond[::-1]:
        ag_arrival(i, k).wait_recv()
    ag_arrival(c, far).wait_recv()
    come(ng, z_arrival(1, whole(bw), aw))
    keep_ug.wait()
    keep_own.wait()
    keep_w.wait()
    for copy in keep_far:
        copy.wait()

    rs_to_relay(c, far).wait_send()
    ag_from_relay(c, far).wait_send()
    for i, k in beyond:
        rs_to_relay(i, k).wait_send()
        ag_from_relay(i, k).wait_send()
    for i, k in near_by:
        rs_direct(i, k).wait_send()
        ag_direct(i, k).wait_send()
    for i in (0, 1):
        rs_relay(i).wait_send()
        ag_to_relay(i).wait_send()
    d_all(0, src1, out1).wait_send()
    d_all(1, src2, out2).wait_send()
    d_all(2, src3, out3).wait_send()
    gone(ny, y_stage(0, whole(users_ref), ucol.at[:, c]))
    swap_users.wait_send()
    gone(2 * ny, s_stage)
    for h in range(parts):
        p_swap(h).wait_send()
    gone(chips, p_stage)
    for m in range(nxc):

        @pl.when(c * nxc + (xch + m) % nxc != x)
        def _():
            u_stage(m).wait_send()

    gone(ng, z_stage(0, by_lead(zw), rw))
    gone(ng, z_stage(1, whole(bw), aw))


def finish(
    devices, ug_hbm, node_hbm, w1_hbm, ug_out, node_out, w1_out,
    ug, node_in, w1_in, node, w1, in_sem, out_sem,
):
    ng, zu, _, width = node_in.shape
    units, (hb, din) = node.shape[0] // 8, w1.shape
    loads = [
        pltpu.make_async_copy(src, dst, in_sem.at[n])
        for n, (src, dst) in enumerate([(node_hbm, node_in), (w1_hbm, w1_in), (ug_hbm, ug)])
    ]
    stores = [
        pltpu.make_async_copy(src, dst, out_sem.at[n])
        for n, (src, dst) in enumerate([(node, node_out), (w1, w1_out), (ug, ug_out)])
    ]
    for load in loads:
        load.start()
    loads[0].wait()
    for o in range(ng):
        lo, hi = min(o * zu, units), min((o + 1) * zu, units)
        if hi > lo:
            part = node_in[o, 0 : hi - lo].astype(F32)
            node[lo * 8 : hi * 8] = part.reshape((hi - lo) * 8, width)
    stores[0].start()
    loads[2].wait()
    stores[2].start()
    loads[1].wait()
    per = w1_in.shape[1] // 16
    for n, (a, c) in enumerate(w1_tiles(hb, din)):
        part = w1_in[n // per, (n % per) * 16 : (n % per) * 16 + 16].astype(F32)
        w1[a * 16 : a * 16 + 16, c * 128 : (c + 1) * 128] = part / devices
    stores[1].start()
    for store in stores:
        store.wait()


def w1_tiles(hb, din):
    return [(a, c) for a in range(hb // 16) for c in range(din // 128)]


def local(ng, shards, users, node_ids, node_table, w_in, b_in, w_out, logit_grad):
    nx = 8 if shards > 8 and shards % 8 == 0 else 2
    ny = shards // nx
    rows, per_row = node_ids.shape
    du = users.shape[1]
    nodes, width = node_table.shape
    din, hid = w_in.shape
    pairs = rows * per_row
    padded = -(-pairs // 128) * 128
    slots = shards * SLOTS
    hb = hid // shards
    zu = -(-nodes // (ng * 8))
    nxc = nx // 2
    far = ng // 2 + 1
    block = (zu, 8, width)
    zt = -(-len(w1_tiles(hb, din)) // ng) * 16
    hbm = pl.BlockSpec(memory_space=pltpu.HBM)

    parts = pl.pallas_call(
        functools.partial(kernel, ny, nx, ng),
        out_shape=(
            jax.ShapeDtypeStruct((rows, du), F32),
            jax.ShapeDtypeStruct((ng, *block), BF16),
            jax.ShapeDtypeStruct((ng, zt, 128), BF16),
        ),
        in_specs=[hbm] * 7,
        out_specs=(hbm, hbm, hbm),
        scratch_shapes=[
            pltpu.VMEM((rows, per_row), jnp.int32),
            pltpu.VMEM((rows, du), BF16),
            pltpu.VMEM((rows, per_row), F32),
            pltpu.VMEM((1, hid), F32),
            pltpu.VMEM((1, hid), F32),
            pltpu.VMEM((nodes, width), BF16),
            pltpu.VMEM((din, hid), BF16),
            pltpu.VMEM((padded, slots), BF16),
            pltpu.VMEM((slots, padded), BF16),
            pltpu.VMEM((nodes, slots), BF16),
            pltpu.VMEM((rows, hid), F32),
            pltpu.VMEM((pairs, hid), BF16),
            pltpu.VMEM((slots, 128), F32),
            pltpu.VMEM((slots, shards), BF16),
            pltpu.VMEM((rows, du), F32),
            *[pltpu.VMEM((shards, 1, 128), F32)] * 2,
            *[pltpu.VMEM((shards, SLOTS, width), BF16)] * 4,
            pltpu.VMEM((ny, 2, rows, du), BF16),
            *[pltpu.VMEM((2 * ny, rows, nxc * hb), BF16)] * 2,
            *[pltpu.VMEM((nxc, hb, du), BF16)] * 2,
            pltpu.VMEM((2, ny, nxc, hb, width), BF16),
            pltpu.VMEM((ny, nxc, hb, width), BF16),
            *[pltpu.VMEM((ny * nxc, hb, width), BF16)] * 2,
            pltpu.VMEM((ng, *block), BF16),
            *[pltpu.VMEM((2, far, *block), BF16)] * 2,
            pltpu.VMEM((2, *block), BF16),
            pltpu.VMEM(block, BF16),
            pltpu.VMEM((2, *block), BF16),
            pltpu.VMEM((ng, zt, 128), BF16),
            pltpu.VMEM((ng, zt, 128), BF16),
            pltpu.VMEM((zt, 128), BF16),
            pltpu.SemaphoreType.DMA((7,)),
            pltpu.SemaphoreType.DMA((4,)),
            *[pltpu.SemaphoreType.DMA((3,))] * 2,
            *[pltpu.SemaphoreType.DMA((1, ny))] * 2,
            *[pltpu.SemaphoreType.DMA((3,))] * 2,
            *[pltpu.SemaphoreType.DMA((2 * ny,))] * 2,
            *[pltpu.SemaphoreType.DMA((nxc,))] * 2,
            *[pltpu.SemaphoreType.DMA((ny * nxc,))] * 2,
            *[pltpu.SemaphoreType.DMA((2, ng))] * 2,
            *[pltpu.SemaphoreType.DMA((2, 2, far))] * 2,
        ],
        compiler_params=pltpu.CompilerParams(
            collective_id=0, has_side_effects=True, vmem_limit_bytes=60 * 2**20
        ),
    )(
        node_ids, users, logit_grad, b_in.reshape(1, hid), w_out.reshape(1, hid),
        node_table, w_in,
    )
    return pl.pallas_call(
        functools.partial(finish, float(shards * ng)),
        out_shape=(
            jax.ShapeDtypeStruct((rows, du), F32),
            jax.ShapeDtypeStruct((nodes, width), F32),
            jax.ShapeDtypeStruct((hb, din), F32),
        ),
        in_specs=[hbm] * 3,
        out_specs=(hbm, hbm, hbm),
        scratch_shapes=[
            pltpu.VMEM((rows, du), F32),
            pltpu.VMEM((ng, *block), BF16),
            pltpu.VMEM((ng, zt, 128), BF16),
            pltpu.VMEM((nodes, width), F32),
            pltpu.VMEM((hb, din), F32),
            pltpu.SemaphoreType.DMA((3,)),
            pltpu.SemaphoreType.DMA((3,)),
        ],
        compiler_params=pltpu.CompilerParams(vmem_limit_bytes=60 * 2**20),
    )(*parts)


def solution(mesh):
    ng, shards = mesh.shape["grp"], mesh.shape["sub"]
    return jax.shard_map(
        functools.partial(local, ng, shards),
        mesh=mesh,
        in_specs=(
            P(("grp", "sub"), None),
            P(("grp", "sub"), None),
            P("sub", None),
            P(),
            P(),
            P(),
            P(("grp", "sub"), None),
        ),
        out_specs=(P(("grp", "sub"), None), P("sub", None), P("sub", None)),
        check_vma=False,
    )
```

```python
import functools

import jax
import jax.numpy as jnp
from jax import lax
from jax.experimental import pallas as pl
from jax.experimental.pallas import tpu as pltpu
from jax.sharding import PartitionSpec as P

F32 = jnp.float32
BF16 = jnp.bfloat16
SLOTS = 8


def dot(a, b, ca=1, cb=0):
    return lax.dot_general(a, b, (((ca,), (cb,)), ((), ())), preferred_element_type=F32)


def iota(shape, dim):
    return lax.broadcasted_iota(jnp.int32, shape, dim)


def each(n, fn):
    group = 7 if n > 8 and (n - 1) % 7 == 0 else 1

    def step(i, carry):
        for j in range(group):
            fn(i * group + j + 1)
        return carry

    lax.fori_loop(0, (n - 1) // group, step, 0)


def push(src, dst, send_sem, recv_sem, device):
    return pltpu.make_async_remote_copy(
        src_ref=src,
        dst_ref=dst,
        send_sem=send_sem,
        recv_sem=recv_sem,
        device_id=device,
        device_id_type=pl.DeviceIdType.MESH,
    )


def kernel(
    ny, nx, ng,
    ids_hbm, users_hbm, lg_hbm, b_hbm, wout_hbm, table_hbm, win_hbm,
    ug_out, anode, aw,
    ids_ref, users_ref, lg_ref, b_ref, wout_ref, table, win,
    place, place_t, select_t, base, pgs, weights, spread, ug,
    src1, out1, src2, out2, src3, out3,
    ucol, ssend, srecv, qusend, qurecv, psend, pswap, pdir, pin,
    znode, rrel, rdir, hsum, bnode, afar, zw, rw, bw,
    load_sem, own_sem, d_send, d_recv, y_send, y_recv, c_send, c_recv, s_send, s_recv,
    u_send, u_recv, p_send, p_recv, z_send, z_recv, zn_send, zn_recv,
):
    rows, per_row = ids_ref.shape
    nodes = table.shape[0]
    width = table.shape[1]
    hid = win.shape[1]
    du = users_ref.shape[1]
    pairs = rows * per_row
    padded = place.shape[0]
    slots = place.shape[1]
    shards = ny * nx
    hb = hid // shards
    band = nx * hb

    g = lax.axis_index("grp")
    me = lax.axis_index("sub")
    y = me // nx
    x = me % nx
    c = x % 2
    xch = x // 2
    nxc = nx // 2
    chips = ny * nxc
    chip = me // 2
    q = y * 2 + c

    loads = [
        pltpu.make_async_copy(src, dst, load_sem.at[n])
        for n, (src, dst) in enumerate(
            [
                (ids_hbm, ids_ref),
                (users_hbm, users_ref),
                (win_hbm, win),
                (table_hbm, table),
                (b_hbm, b_ref),
                (wout_hbm, wout_ref),
                (lg_hbm, lg_ref),
            ]
        )
    ]
    for load in loads:
        load.start()
    load_ids, load_users, load_win, load_table, *load_small = loads

    def y_peer(d):
        return {"sub": ((y + d) % ny) * nx + x}

    partner = {"sub": chip * 2 + 1 - c}

    def sub_peer(d):
        return {"sub": (me + d) % shards}

    def z_peer(d):
        return {"grp": (g + d) % ng}

    barrier = pltpu.get_barrier_semaphore()

    def greet(peer):
        def go(d):
            pl.semaphore_signal(
                barrier, inc=1, device_id=peer(d), device_id_type=pl.DeviceIdType.MESH
            )

        return go

    each(shards, greet(sub_peer))
    each(ng, greet(z_peer))

    lanes = 128
    half = lanes // 2
    before = (iota((padded, padded), 0) > iota((padded, padded), 1)).astype(F32).astype(BF16)
    slot_row = iota((slots, lanes), 0) % SLOTS
    slot_col = iota((slots, lanes), 1)
    weight = jnp.where(slot_col == slot_row, 32.0, 0.0)
    weights[...] = weight + jnp.where(slot_col == slot_row + half, 1.0, 0.0)
    spread[...] = (
        (iota((slots, shards), 0) // SLOTS == iota((slots, shards), 1)).astype(F32).astype(BF16)
    )
    load_ids.wait()
    ids = ids_ref[...]
    cols = jnp.concatenate(
        [jnp.broadcast_to(ids[:, k : k + 1], (rows, lanes)) for k in range(per_row)]
        + [jnp.full((padded - pairs, lanes), -1, jnp.int32)],
        axis=0,
    )
    shift = nodes.bit_length() - 1
    owner = lax.shift_right_arithmetic(cols, jnp.int32(shift))
    local = cols & (nodes - 1)
    lane = iota((padded, lanes), 1)
    hit = (owner == lane).astype(F32)
    hit_low = hit.astype(BF16)
    rank = jnp.sum(dot(before, hit_low) * hit, axis=1, keepdims=True)
    slot_lane = rank.astype(jnp.int32)
    high, low = lax.shift_right_arithmetic(local, jnp.int32(5)) + 1, local & 31
    asked = jnp.where(lane == slot_lane, high, jnp.where(lane == slot_lane + half, low, 0))
    request = dot(hit_low, asked.astype(F32).astype(BF16), 0, 0)
    src1[...] = request[0:shards].reshape(shards, 1, lanes)

    pl.semaphore_wait(barrier, (shards - 1) + (ng - 1))

    def y_stage(num, src, dst):
        return lambda d: push(
            src((y + d) % ny), dst.at[y], y_send.at[num, d], y_recv.at[num, d], y_peer(d)
        )

    def y_arrival(num, src, dst):
        return lambda d: push(
            src(y), dst.at[(y + ny - d) % ny], y_send.at[num, d], y_recv.at[num, d], y_peer(d)
        )

    def z_stage(num, src, dst):
        return lambda d: push(
            src((g + d) % ng), dst.at[g], z_send.at[num, d], z_recv.at[num, d], z_peer(d)
        )

    def z_arrival(num, src, dst):
        return lambda d: push(
            src(g), dst.at[(g + ng - d) % ng], z_send.at[num, d], z_recv.at[num, d], z_peer(d)
        )

    def send_all(num, src, dst):
        def one(t):
            push(src.at[t], dst.at[me], d_send.at[num], d_recv.at[num], {"sub": t}).start()

        def row(i, carry):
            dy = ny // 2 + ((i + 1) // 2) * (1 - 2 * (i % 2))
            for dx in range(nx):
                one(((y + dy) % ny) * nx + (x + dx) % nx)
            return carry

        lax.fori_loop(0, ny - 1, row, 0)
        for dx in range(1, nx):
            one(y * nx + (x + dx) % nx)

    def d_all(num, src, dst):
        rest = pl.ds(0, shards - 1)
        return push(src.at[rest], dst.at[rest], d_send.at[num], d_recv.at[num], sub_peer(1))

    def go(n, make):
        each(n, lambda d: make(d).start())

    def come(n, make):
        each(n, lambda d: make(d).wait_recv())

    def gone(n, make):
        each(n, lambda d: make(d).wait_send())

    def by_lead(ref):
        return lambda t: ref.at[t]

    def whole(ref):
        return lambda t: ref

    send_all(0, src1, out1)
    out1[me] = src1[me]

    load_users.wait()
    ucol[y, c] = users_ref[...]
    load_win.wait()
    for load in load_small:
        load.wait()
    base[...] = dot(users_ref[...], win[0:du, :]) + b_ref[...]
    load_table.wait()
    d_all(0, src1, out1).wait_recv()

    wanted = dot(spread[...], out1[...].reshape(shards, lanes).astype(BF16))
    place_of = jnp.sum(wanted * weights[...], axis=1, keepdims=True) - 32.0
    select = (iota((slots, nodes), 1).astype(F32) == place_of).astype(F32)
    fetched = dot(select.astype(BF16), table[...])
    src2[...] = fetched.reshape(shards, SLOTS, width).astype(BF16)
    send_all(1, src2, out2)
    out2[me] = src2[me]
    place_row = jnp.broadcast_to(place_of, (slots, lanes)).T[0:1]
    select_t[...] = (iota((nodes, slots), 0).astype(F32) == place_row).astype(F32).astype(BF16)
    code = owner.astype(F32) * float(SLOTS) + rank
    chosen = (iota((padded, slots), 1).astype(F32) == code[:, 0:1]).astype(F32)
    place[...] = chosen.astype(BF16)
    code_row = code.T[0:1]
    place_t[...] = (iota((slots, padded), 0).astype(F32) == code_row).astype(F32).astype(BF16)
    go(ny, y_stage(0, whole(users_ref), ucol.at[:, c]))
    d_all(1, src2, out2).wait_recv()

    returned = out2[...].astype(F32).reshape(slots, width).astype(BF16)
    pn = dot(place[0:pairs, :], returned).astype(BF16)
    grad_col = jnp.concatenate([lg_ref[:, k : k + 1] for k in range(per_row)], axis=0)
    step = min(hid, 512)
    sums = []
    for left in range(0, hid, step):
        cut = slice(left, left + step)
        part = dot(pn, win[du:, cut]).reshape(per_row, rows, step)
        pre = (part + base[:, cut][None]).reshape(pairs, step)
        squash = jax.nn.sigmoid(pre)
        pre_grad = (
            (grad_col * wout_ref[:, cut]) * (squash * (1.0 + pre * (1.0 - squash)))
        ).astype(BF16)
        pgs[:, cut] = pre_grad
        sums.append(jnp.sum(pre_grad.astype(F32).reshape(per_row, rows, step), axis=0))
    in_grad = dot(pgs[...], win[du:, :], 1, 1).astype(BF16)
    back = dot(place_t[:, 0:pairs], in_grad)

    src3[...] = back.reshape(shards, SLOTS, width).astype(BF16)
    send_all(2, src3, out3)
    out3[me] = src3[me]

    come(ny, y_arrival(0, whole(users_ref), ucol.at[:, c]))
    swap_users = push(ucol.at[:, c], ucol.at[:, c], c_send.at[0], c_recv.at[0], partner)
    swap_users.start()
    row_sum = jnp.concatenate(sums, axis=1)
    bh = band // 2
    for i in range(2 * ny):
        ssend[i] = row_sum[:, i * bh : (i + 1) * bh].astype(BF16)

    def s_stage(d):
        t = (q + d) % (2 * ny)
        return push(
            ssend.at[t], srecv.at[q], s_send.at[d], s_recv.at[d],
            {"sub": (t // 2) * nx + xch * 2 + t % 2},
        )

    def s_arrival(d):
        return push(
            ssend.at[q], srecv.at[(q + 2 * ny - d) % (2 * ny)], s_send.at[d], s_recv.at[d], partner
        )

    go(2 * ny, s_stage)
    srecv[q] = ssend[q]

    pn_t = pn.astype(F32).T.astype(BF16)
    parts = 2 if ny % 2 == 0 else 1
    bands = ny // parts

    def p_swap(h):
        part = slice(h * bands, (h + 1) * bands)
        return push(
            psend.at[1 - c, part], pswap.at[part], c_send.at[1 + h], c_recv.at[1 + h], partner
        )

    for h in range(parts):
        for j in range(h * bands, (h + 1) * bands):
            prod = dot(pn_t, pgs[:, j * band : (j + 1) * band]).T.astype(BF16)
            for i in range(nx):
                psend[i % 2, j, i // 2] = prod[i * hb : (i + 1) * hb]
        p_swap(h).start()
    for h in range(parts):
        p_swap(h).wait_recv()
        part = slice(h * bands, (h + 1) * bands)
        mine = psend[c, part].astype(F32) + pswap[part].astype(F32)
        pdir[h * bands * nxc : (h + 1) * bands * nxc] = mine.reshape(
            bands * nxc, hb, width
        ).astype(BF16)

    def p_stage(d):
        t = (chip + d) % chips
        return push(pdir.at[t], pin.at[chip], p_send, p_recv, {"sub": t * 2 + c})

    def p_all():
        rest = pl.ds(0, chips - 1)
        return push(pdir.at[rest], pin.at[rest], p_send, p_recv, partner)

    go(chips, p_stage)
    pin[chip] = pdir[chip]

    swap_users.wait_recv()
    come(2 * ny, s_arrival)
    user_cols = dot(
        srecv[...].reshape(2 * ny * rows, bh), ucol[...].reshape(2 * ny * rows, du), 0, 0
    ).astype(BF16)
    for m in range(nxc):
        qusend[m] = user_cols[m * hb : (m + 1) * hb]

    def u_stage(m):
        at = (xch + m) % nxc
        return push(
            qusend.at[at], qurecv.at[xch], u_send.at[at], u_recv.at[xch],
            {"sub": y * nx + c * nxc + at},
        )

    def u_arrival(i):
        return push(qusend.at[0], qurecv.at[i], u_send.at[0], u_recv.at[i], partner)

    for m in range(nxc):
        at = (xch + m) % nxc

        @pl.when(c * nxc + at != x)
        def _():
            u_stage(m).start()

        @pl.when(c * nxc + at == x)
        def _():
            qurecv[xch] = qusend[at]

    d_all(2, src3, out3).wait_recv()
    arrived = out3[...].astype(F32).reshape(slots, width).astype(BF16)
    node_part = dot(select_t[...], arrived).reshape(nodes // 8, 8, width).astype(BF16)
    zu = znode.shape[1]
    units = nodes // 8
    for o in range(ng):
        lo, hi = min(o * zu, units), min((o + 1) * zu, units)
        if hi > lo:
            znode[o, 0 : hi - lo] = node_part[lo:hi]
        if hi - lo < zu:
            znode[o, hi - lo :] = jnp.zeros((zu - (hi - lo), 8, width), BF16)
    far = ng // 2
    relay = far // 2
    near_by = [(i, k) for k in range(relay - 1, 0, -1) for i in (0, 1)]
    beyond = [(i, k) for k in range(far - 1, relay, -1) for i in (0, 1)]

    def off(i, k):
        return (g + k * (1 - 2 * i) + ng) % ng

    def z_push(phase, i, k, src, dst, hop):
        return push(
            src, dst, zn_send.at[phase, i, k], zn_recv.at[phase, i, k], {"grp": off(i, hop)}
        )

    def rs_to_relay(i, k):
        return z_push(0, i, k, znode.at[off(i, -k)], rrel.at[i, k], relay - k)

    def rs_direct(i, k):
        return z_push(0, i, k, znode.at[off(i, -k)], rdir.at[i, k], -k)

    def rs_relay(i):
        return z_push(0, i, relay, hsum.at[i], rdir.at[i, relay], -relay)

    def ag_direct(i, k):
        return z_push(1, i, k, bnode, anode.at[g], k)

    def ag_to_relay(i):
        return z_push(1, i, relay, bnode, afar.at[i], relay)

    def ag_from_relay(i, k):
        return z_push(1, i, k, afar.at[i], anode.at[off(i, -relay)], k - relay)

    def ag_arrival(i, k):
        return z_push(1, i, k, bnode, anode.at[off(i, -k)], k)

    rs_to_relay(c, far).start()
    for i, k in beyond:
        rs_to_relay(i, k).start()
    for i, k in near_by:
        rs_direct(i, k).start()

    p_all().wait_recv()
    for m in range(nxc):

        @pl.when(m * 2 + x // nxc != x)
        def _():
            u_arrival(m).wait_recv()

    user_block = qurecv[0].astype(F32)
    for j in range(1, nxc):
        user_block = user_block + qurecv[j].astype(F32)
    node_block = pin[0].astype(F32)
    for j in range(1, chips):
        node_block = node_block + pin[j].astype(F32)
    block = jnp.concatenate([user_block, node_block], axis=1).astype(BF16)
    tiles = w1_tiles(hb, du + width)
    per = zw.shape[1] // 16
    for n in range(ng * per):
        at = (n // per, slice((n % per) * 16, (n % per) * 16 + 16))
        if n < len(tiles):
            down, over = tiles[n]
            zw[at] = block[down * 16 : down * 16 + 16, over * lanes : (over + 1) * lanes]
        else:
            zw[at] = jnp.zeros((16, lanes), BF16)
    go(ng, z_stage(0, by_lead(zw), rw))
    rw[g] = zw[g]

    for turn in (1, 0):
        i = (c + turn) % 2
        part = znode[off(i, -relay)].astype(F32)
        for k in range(relay + 1, far + (1 - turn)):
            rs_to_relay(i, k).wait_recv()
            part = part + rrel[i, k].astype(F32)
        hsum[i] = part.astype(BF16)
        rs_relay(i).start()

    mine = znode[g].astype(F32)
    for i, k in [(i, k) for k in range(1, relay + 1) for i in (0, 1)]:
        rs_direct(i, k).wait_recv()
        mine = mine + rdir[i, k].astype(F32)
    bnode[...] = mine.astype(BF16)
    for i in (0, 1):
        ag_to_relay(i).start()
    for i, k in near_by:
        ag_direct(i, k).start()
    keep_own = pltpu.make_async_copy(bnode, anode.at[g], own_sem.at[0])
    keep_own.start()

    come(ng, z_arrival(0, by_lead(zw), rw))
    tile_sum = rw[0].astype(F32)
    for j in range(1, ng):
        tile_sum = tile_sum + rw[j].astype(F32)
    bw[...] = tile_sum.astype(BF16)
    go(ng, z_stage(1, whole(bw), aw))
    keep_w = pltpu.make_async_copy(bw, aw.at[g], own_sem.at[1])
    keep_w.start()

    keep_far = []
    for turn in (0, 1):
        i = (c + turn) % 2
        ag_to_relay(i).wait_recv()
        for k in range(far - turn, relay, -1):
            ag_from_relay(i, k).start()
        copy = pltpu.make_async_copy(afar.at[i], anode.at[off(i, -relay)], own_sem.at[2 + turn])
        copy.start()
        keep_far.append(copy)

    ug[...] = dot(row_sum.astype(BF16), win[0:du, :], 1, 1)
    keep_ug = pltpu.make_async_copy(ug, ug_out, load_sem.at[0])
    keep_ug.start()
    for i, k in near_by[::-1] + beyond[::-1]:
        ag_arrival(i, k).wait_recv()
    ag_arrival(c, far).wait_recv()
    come(ng, z_arrival(1, whole(bw), aw))
    keep_ug.wait()
    keep_own.wait()
    keep_w.wait()
    for copy in keep_far:
        copy.wait()

    rs_to_relay(c, far).wait_send()
    ag_from_relay(c, far).wait_send()
    for i, k in beyond:
        rs_to_relay(i, k).wait_send()
        ag_from_relay(i, k).wait_send()
    for i, k in near_by:
        rs_direct(i, k).wait_send()
        ag_direct(i, k).wait_send()
    for i in (0, 1):
        rs_relay(i).wait_send()
        ag_to_relay(i).wait_send()
    d_all(0, src1, out1).wait_send()
    d_all(1, src2, out2).wait_send()
    d_all(2, src3, out3).wait_send()
    gone(ny, y_stage(0, whole(users_ref), ucol.at[:, c]))
    swap_users.wait_send()
    gone(2 * ny, s_stage)
    for h in range(parts):
        p_swap(h).wait_send()
    p_all().wait_send()
    for m in range(nxc):

        @pl.when(c * nxc + (xch + m) % nxc != x)
        def _():
            u_stage(m).wait_send()

    gone(ng, z_stage(0, by_lead(zw), rw))
    gone(ng, z_stage(1, whole(bw), aw))


def finish(
    devices, ug_hbm, node_hbm, w1_hbm, ug_out, node_out, w1_out,
    ug, node_in, w1_in, node, w1, in_sem, out_sem,
):
    ng, zu, _, width = node_in.shape
    units, (hb, din) = node.shape[0] // 8, w1.shape
    loads = [
        pltpu.make_async_copy(src, dst, in_sem.at[n])
        for n, (src, dst) in enumerate([(node_hbm, node_in), (w1_hbm, w1_in), (ug_hbm, ug)])
    ]
    stores = [
        pltpu.make_async_copy(src, dst, out_sem.at[n])
        for n, (src, dst) in enumerate([(node, node_out), (w1, w1_out), (ug, ug_out)])
    ]
    for load in loads:
        load.start()
    loads[0].wait()
    for o in range(ng):
        lo, hi = min(o * zu, units), min((o + 1) * zu, units)
        if hi > lo:
            part = node_in[o, 0 : hi - lo].astype(F32)
            node[lo * 8 : hi * 8] = part.reshape((hi - lo) * 8, width)
    stores[0].start()
    loads[2].wait()
    stores[2].start()
    loads[1].wait()
    per = w1_in.shape[1] // 16
    for n, (a, c) in enumerate(w1_tiles(hb, din)):
        part = w1_in[n // per, (n % per) * 16 : (n % per) * 16 + 16].astype(F32)
        w1[a * 16 : a * 16 + 16, c * 128 : (c + 1) * 128] = part / devices
    stores[1].start()
    for store in stores:
        store.wait()


def w1_tiles(hb, din):
    return [(a, c) for a in range(hb // 16) for c in range(din // 128)]


def local(ng, shards, users, node_ids, node_table, w_in, b_in, w_out, logit_grad):
    nx = 8 if shards > 8 and shards % 8 == 0 else 2
    ny = shards // nx
    rows, per_row = node_ids.shape
    du = users.shape[1]
    nodes, width = node_table.shape
    din, hid = w_in.shape
    pairs = rows * per_row
    padded = -(-pairs // 128) * 128
    slots = shards * SLOTS
    hb = hid // shards
    zu = -(-nodes // (ng * 8))
    nxc = nx // 2
    far = ng // 2 + 1
    block = (zu, 8, width)
    zt = -(-len(w1_tiles(hb, din)) // ng) * 16
    hbm = pl.BlockSpec(memory_space=pltpu.HBM)

    parts = pl.pallas_call(
        functools.partial(kernel, ny, nx, ng),
        out_shape=(
            jax.ShapeDtypeStruct((rows, du), F32),
            jax.ShapeDtypeStruct((ng, *block), BF16),
            jax.ShapeDtypeStruct((ng, zt, 128), BF16),
        ),
        in_specs=[hbm] * 7,
        out_specs=(hbm, hbm, hbm),
        scratch_shapes=[
            pltpu.VMEM((rows, per_row), jnp.int32),
            pltpu.VMEM((rows, du), BF16),
            pltpu.VMEM((rows, per_row), F32),
            pltpu.VMEM((1, hid), F32),
            pltpu.VMEM((1, hid), F32),
            pltpu.VMEM((nodes, width), BF16),
            pltpu.VMEM((din, hid), BF16),
            pltpu.VMEM((padded, slots), BF16),
            pltpu.VMEM((slots, padded), BF16),
            pltpu.VMEM((nodes, slots), BF16),
            pltpu.VMEM((rows, hid), F32),
            pltpu.VMEM((pairs, hid), BF16),
            pltpu.VMEM((slots, 128), F32),
            pltpu.VMEM((slots, shards), BF16),
            pltpu.VMEM((rows, du), F32),
            *[pltpu.VMEM((shards, 1, 128), F32)] * 2,
            *[pltpu.VMEM((shards, SLOTS, width), BF16)] * 4,
            pltpu.VMEM((ny, 2, rows, du), BF16),
            *[pltpu.VMEM((2 * ny, rows, nxc * hb), BF16)] * 2,
            *[pltpu.VMEM((nxc, hb, du), BF16)] * 2,
            pltpu.VMEM((2, ny, nxc, hb, width), BF16),
            pltpu.VMEM((ny, nxc, hb, width), BF16),
            *[pltpu.VMEM((ny * nxc, hb, width), BF16)] * 2,
            pltpu.VMEM((ng, *block), BF16),
            *[pltpu.VMEM((2, far, *block), BF16)] * 2,
            pltpu.VMEM((2, *block), BF16),
            pltpu.VMEM(block, BF16),
            pltpu.VMEM((2, *block), BF16),
            pltpu.VMEM((ng, zt, 128), BF16),
            pltpu.VMEM((ng, zt, 128), BF16),
            pltpu.VMEM((zt, 128), BF16),
            pltpu.SemaphoreType.DMA((7,)),
            pltpu.SemaphoreType.DMA((4,)),
            *[pltpu.SemaphoreType.DMA((3,))] * 2,
            *[pltpu.SemaphoreType.DMA((1, ny))] * 2,
            *[pltpu.SemaphoreType.DMA((3,))] * 2,
            *[pltpu.SemaphoreType.DMA((2 * ny,))] * 2,
            *[pltpu.SemaphoreType.DMA((nxc,))] * 2,
            *[pltpu.SemaphoreType.DMA] * 2,
            *[pltpu.SemaphoreType.DMA((2, ng))] * 2,
            *[pltpu.SemaphoreType.DMA((2, 2, far))] * 2,
        ],
        compiler_params=pltpu.CompilerParams(
            collective_id=0, has_side_effects=True, vmem_limit_bytes=60 * 2**20
        ),
    )(
        node_ids, users, logit_grad, b_in.reshape(1, hid), w_out.reshape(1, hid),
        node_table, w_in,
    )
    return pl.pallas_call(
        functools.partial(finish, float(shards * ng)),
        out_shape=(
            jax.ShapeDtypeStruct((rows, du), F32),
            jax.ShapeDtypeStruct((nodes, width), F32),
            jax.ShapeDtypeStruct((hb, din), F32),
        ),
        in_specs=[hbm] * 3,
        out_specs=(hbm, hbm, hbm),
        scratch_shapes=[
            pltpu.VMEM((rows, du), F32),
            pltpu.VMEM((ng, *block), BF16),
            pltpu.VMEM((ng, zt, 128), BF16),
            pltpu.VMEM((nodes, width), F32),
            pltpu.VMEM((hb, din), F32),
            pltpu.SemaphoreType.DMA((3,)),
            pltpu.SemaphoreType.DMA((3,)),
        ],
        compiler_params=pltpu.CompilerParams(vmem_limit_bytes=60 * 2**20),
    )(*parts)


def solution(mesh):
    ng, shards = mesh.shape["grp"], mesh.shape["sub"]
    return jax.shard_map(
        functools.partial(local, ng, shards),
        mesh=mesh,
        in_specs=(
            P(("grp", "sub"), None),
            P(("grp", "sub"), None),
            P("sub", None),
            P(),
            P(),
            P(),
            P(("grp", "sub"), None),
        ),
        out_specs=(P(("grp", "sub"), None), P("sub", None), P("sub", None)),
        check_vma=False,
    )
```
